32 devices in a mesh: gx: 8 (over y, x, core), gy: 4 (over z).
Axes of the slice: x: 2, y: 2, z: 4, core: 2. Of those that a mesh axis runs over, the one named last changes fastest.
Arguments:
- density: float32 [8192, 8192], P('gy', 'gx'), may hold values from -6 to 6
- kernel_rows: float32 [8192], P('gy'), may hold values from 0.1 to 1
- kernel_cols: float32 [8192], P('gx'), may hold values from 0.1 to 1
Outputs:
- spectrum_real: float32 [8192, 8192], P('gy', 'gx')
- spectrum_imag: float32 [8192, 8192], P('gy', 'gx')
The draws below stay inside these ranges and needn't reach their ends.
All inputs are finite; a program needn't handle non-finite values.
Results may differ from the reference program's by a relative error of at most 0.000071.
Values sent between devices are 32-bit elements; how exact they have to be, the bound alone decides.
A program may use at most 384 MiB of HBM per device.

```python
import math
import jax
import jax.numpy as jnp

NR = 8192
NC = 8192


def block_scale(own_key, extent, cuts, smallest, top_value):
    factor_of = 1.0
    for dim, blocks in cuts:
        heights = jax.random.uniform(jax.random.fold_in(jax.random.fold_in(own_key, 6), dim), (blocks,), jnp.float32, smallest / len(cuts), top_value / len(cuts))
        factor_of = factor_of * jnp.repeat(jnp.exp(heights), extent[dim] // blocks).reshape((-1,) + (1,) * (len(extent) - 1 - dim))
    return factor_of


def normal_values(stream_key, extent, deviation, bound, shards=(), held_as=jnp.bfloat16):
    array = deviation * jax.random.normal(stream_key, extent, jnp.float32)
    if shards:
        array = array * block_scale(stream_key, extent, shards, -0.22, 0.18)
    return jnp.clip(array, -bound, bound).astype(held_as)


def setup_inputs(seed: int = 0) -> dict:
    keys = jax.random.split(jax.random.key(seed), 4)
    density = normal_values(keys[0], (NR, NC), 1.0, 6.0, ((0, 4), (1, 8)), jnp.float32)
    kernel_rows = jnp.clip(jnp.exp(math.log(1.0) - 2.3025851 * jax.random.uniform(keys[1], (NR,), jnp.float32) ** block_scale(keys[1], (NR,), ((0, 4),), -0.2, 0.2)), 0.1, 1.0)
    kernel_cols = jnp.clip(jnp.exp(math.log(1.0) - 2.3025851 * jax.random.uniform(keys[2], (NC,), jnp.float32) ** block_scale(keys[2], (NC,), ((0, 8),), -0.2, 0.2)), 0.1, 1.0)
    return dict(density=density, kernel_rows=kernel_rows, kernel_cols=kernel_cols)


def reference(density, kernel_rows, kernel_cols):
    transform = jnp.fft.fft2(density)
    factor = kernel_rows[:, None] * kernel_cols[None, :] * (1.0 / math.sqrt(NR * NC))
    return (jnp.real(transform) * factor, jnp.imag(transform) * factor)
```

```python
import math

import jax
import jax.numpy as jnp
from jax import lax
from jax.experimental import pallas as pl
from jax.experimental.pallas import tpu as pltpu
from jax.sharding import PartitionSpec as P

NR = 8192
NC = 8192


HIGHEST = lax.Precision.HIGHEST
TWO_PI = 2.0 * math.pi


def dft_tables(length):
    positions = jnp.arange(length, dtype=jnp.int32)
    phase = positions[:, None] * positions[None, :] % length
    phase_angle = phase.astype(jnp.float32) * (-TWO_PI / length)
    return (jnp.cos(phase_angle), jnp.sin(phase_angle))


def rotate_by(real_part, imag_part, cosine, sine_part):
    return (real_part * cosine - imag_part * sine_part, real_part * sine_part + imag_part * cosine)


def rotate_phase(real_part, imag_part, phase, total):
    phase_angle = (phase % total).astype(jnp.float32) * (-TWO_PI / total)
    return rotate_by(real_part, imag_part, jnp.cos(phase_angle), jnp.sin(phase_angle))


def split_length(length):
    inner = 1
    for factor in range(1, length + 1):
        if factor * factor > length:
            break
        if length % factor == 0:
            inner = factor
    return (inner, length // inner)


def whole_columns_dft(real_part):
    rows_here, length = real_part.shape
    inner, outer = split_length(length)
    cos_outer, sin_outer = dft_tables(outer)
    shaped_real = real_part.reshape(rows_here, outer, inner)
    first_real = jnp.einsum("rqp,qk->rkp", shaped_real, cos_outer, precision=HIGHEST)
    first_imag = jnp.einsum("rqp,qk->rkp", shaped_real, sin_outer, precision=HIGHEST)
    phase = (
        jnp.arange(outer, dtype=jnp.int32)[:, None] * jnp.arange(inner, dtype=jnp.int32)[None, :]
    )
    first_real, first_imag = rotate_phase(first_real, first_imag, phase[None, :, :], length)
    cos_inner, sin_inner = dft_tables(inner)
    new_real = jnp.einsum("rkp,pj->rjk", first_real, cos_inner, precision=HIGHEST) - jnp.einsum(
        "rkp,pj->rjk", first_imag, sin_inner, precision=HIGHEST
    )
    new_imag = jnp.einsum("rkp,pj->rjk", first_real, sin_inner, precision=HIGHEST) + jnp.einsum(
        "rkp,pj->rjk", first_imag, cos_inner, precision=HIGHEST
    )
    return (new_real.reshape(rows_here, length), new_imag.reshape(rows_here, length))


def whole_rows_dft(real_part, imag_part):
    length, width_here = real_part.shape
    inner, outer = split_length(length)
    cos_outer, sin_outer = dft_tables(outer)
    shaped_real = real_part.reshape(outer, inner, width_here)
    shaped_imag = imag_part.reshape(outer, inner, width_here)
    first_real = jnp.einsum("qpc,qk->kpc", shaped_real, cos_outer, precision=HIGHEST) - jnp.einsum(
        "qpc,qk->kpc", shaped_imag, sin_outer, precision=HIGHEST
    )
    first_imag = jnp.einsum("qpc,qk->kpc", shaped_real, sin_outer, precision=HIGHEST) + jnp.einsum(
        "qpc,qk->kpc", shaped_imag, cos_outer, precision=HIGHEST
    )
    phase = (
        jnp.arange(outer, dtype=jnp.int32)[:, None] * jnp.arange(inner, dtype=jnp.int32)[None, :]
    )
    first_real, first_imag = rotate_phase(first_real, first_imag, phase[:, :, None], length)
    cos_inner, sin_inner = dft_tables(inner)
    new_real = jnp.einsum("kpc,pj->jkc", first_real, cos_inner, precision=HIGHEST) - jnp.einsum(
        "kpc,pj->jkc", first_imag, sin_inner, precision=HIGHEST
    )
    new_imag = jnp.einsum("kpc,pj->jkc", first_real, sin_inner, precision=HIGHEST) + jnp.einsum(
        "kpc,pj->jkc", first_imag, cos_inner, precision=HIGHEST
    )
    return (new_real.reshape(length, width_here), new_imag.reshape(length, width_here))


def pencil_transform(density):
    rows_here, width_here = density.shape
    row_slab = lax.all_to_all(density, "gx", split_axis=0, concat_axis=1, tiled=True)
    real_part, imag_part = whole_columns_dft(row_slab)
    column_slab = (
        lax.all_to_all(
            lax.all_to_all(real_part, "gx", split_axis=1, concat_axis=0, tiled=True),
            "gy",
            split_axis=1,
            concat_axis=0,
            tiled=True,
        ),
        lax.all_to_all(
            lax.all_to_all(imag_part, "gx", split_axis=1, concat_axis=0, tiled=True),
            "gy",
            split_axis=1,
            concat_axis=0,
            tiled=True,
        ),
    )
    real_part, imag_part = whole_rows_dft(column_slab[0], column_slab[1])
    returned = (
        lax.all_to_all(real_part, "gy", split_axis=0, concat_axis=1, tiled=True),
        lax.all_to_all(imag_part, "gy", split_axis=0, concat_axis=1, tiled=True),
    )
    return (returned[0].reshape(rows_here, width_here), returned[1].reshape(rows_here, width_here))


def on_device(density, kernel_rows, kernel_cols):
    real_part, imag_part = pencil_transform(density)
    factor = kernel_rows[:, None] * kernel_cols[None, :] * (1.0 / math.sqrt(NR * NC))
    return (real_part * factor, imag_part * factor)


RADIX = 32
VMEM = pltpu.VMEM
FULL = pl.BlockSpec(memory_space=pltpu.VMEM)


def unit_angle(index, total):
    angle = (index % total).astype(jnp.float32) * (-TWO_PI / total)
    return (jnp.cos(angle), jnp.sin(angle))


def halves(table):
    high = lax.reduce_precision(table, exponent_bits=8, mantissa_bits=7)
    return (high.astype(jnp.bfloat16), (table - high).astype(jnp.bfloat16))


def times_root(value, index, total):
    real, imag = value
    index = index % total
    if index == 0:
        return value
    if 4 * index == total:
        return (imag, -real) if imag is not None else (None, -real)
    if 2 * index == total:
        return (-real, None if imag is None else -imag)
    cosine = math.cos(TWO_PI * index / total)
    sine = -math.sin(TWO_PI * index / total)
    if imag is None:
        return (real * cosine, real * sine)
    if real is None:
        return (imag * -sine, imag * cosine)
    return (real * cosine - imag * sine, real * sine + imag * cosine)


def plus(left, right):
    if left is None:
        return right
    return left if right is None else left + right


def minus(left, right):
    if right is None:
        return left
    return -right if left is None else left - right


def small_dft(values, needed):
    length = len(values)
    if length == 1:
        return values
    half = length // 2
    keep = min(needed, half)
    even = small_dft(values[0::2], keep)
    odd = small_dft(values[1::2], keep)
    out = [None] * length
    for k in range(keep):
        turned = times_root(odd[k], k, length)
        out[k] = (plus(even[k][0], turned[0]), plus(even[k][1], turned[1]))
        out[k + half] = (minus(even[k][0], turned[0]), minus(even[k][1], turned[1]))
    return out


def real_dft(values):
    length = len(values)
    if length == 1:
        return [(values[0], None)]
    half = length // 2
    even = real_dft(values[0::2])
    odd = real_dft(values[1::2])
    out = [None] * (half + 1)

    def entry(spectrum, k):
        if k < len(spectrum):
            return spectrum[k]
        real, imag = spectrum[half - k]
        return (real, None if imag is None else -imag)

    for k in range(half + 1):
        if k == half:
            e, o = even[0], odd[0]
            out[k] = (minus(e[0], o[0]), None)
        else:
            turned = times_root(entry(odd, k), k, length)
            e = entry(even, k)
            out[k] = (plus(e[0], turned[0]), plus(e[1], turned[1]))
    return out


def product(left_high, left_low, right_high, right_low):
    dot = lambda a, b: jnp.dot(a, b, preferred_element_type=jnp.float32)
    return dot(left_high, right_high) + dot(left_high, right_low) + dot(left_low, right_high)


def split_store(high_ref, low_ref, place, value):
    high = value.astype(jnp.bfloat16)
    high_ref[place] = high
    low_ref[place] = (value - high.astype(jnp.float32)).astype(jnp.bfloat16)


def rows_kernel(flag, own, near, end, far, cosine, sine, table_high, table_low, kept, sent, high, low):
    depth = cosine.shape[1]
    width = own.shape[1]
    per_block = own.shape[0] // depth
    count = RADIX // 2 + 1
    quarter = table_high.shape[0] // 8
    upper = flag[0] > 0

    @pl.loop(0, depth // 16)
    def _(step):
        start = pl.multiple_of(step * 16, 16)
        for lane in range(0, width, 128):
            lanes = pl.ds(lane, 128)

            def take(ref, q):
                return ref[pl.ds(pl.multiple_of(q * depth + start, 16), 16), lanes]

            blocks = []
            for first, second in ((end, far), (own, near), (near, own), (far, end)):
                for q in range(per_block):
                    blocks.append(jnp.where(upper, take(second, q), take(first, q)))
            spectrum = real_dft(blocks)
            for k in range(count):
                real, imag = spectrum[k]
                if k:
                    c = cosine[k, pl.ds(start, 16), :]
                    s = sine[k, pl.ds(start, 16), :]
                    if imag is None:
                        real, imag = real * c, real * s
                    else:
                        real, imag = real * c - imag * s, real * s + imag * c
                if imag is None:
                    imag = jnp.zeros_like(real)
                split_store(high, low, (k, pl.ds(start, 16), lanes), real)
                split_store(high, low, (k, pl.ds(pl.multiple_of(depth + start, 16), 16), lanes), imag)

    def put(k, result):
        rows = pl.ds(pl.multiple_of(k * quarter, 8), quarter)
        kept[0, rows, :] = result[0:quarter]
        kept[1, rows, :] = result[quarter : 2 * quarter]
        sent[0, rows, :] = result[2 * quarter : 3 * quarter]
        sent[1, rows, :] = result[3 * quarter : 4 * quarter]

    direct = pl.ds(0, 4 * quarter)
    for k in (0, RADIX // 2):
        put(k, product(table_high[direct, :], table_low[direct, :], high[k], low[k]))

    @pl.loop(1, RADIX // 2)
    def _(k):
        result = product(table_high[...], table_low[...], high[k], low[k])
        put(k, result[: 4 * quarter])
        put(RADIX - k, result[4 * quarter :])


def rows_stage(flag, own, near, end, far, tables):
    length, width = own.shape
    depth = tables[0].shape[1]
    shape = jax.ShapeDtypeStruct((2, length, width), jnp.float32)
    count = RADIX // 2 + 1
    return pl.pallas_call(
        rows_kernel,
        out_shape=(shape, shape),
        in_specs=[pl.BlockSpec(memory_space=pltpu.SMEM)] + [FULL] * 8,
        out_specs=(FULL, FULL),
        scratch_shapes=[
            VMEM((count, 2 * depth, width), jnp.bfloat16),
            VMEM((count, 2 * depth, width), jnp.bfloat16),
        ],
        compiler_params=pltpu.CompilerParams(vmem_limit_bytes=56 * 2**20),
        cost_estimate=pl.CostEstimate(
            flops=30 * 10**9, bytes_accessed=24 * 2**20, transcendentals=0
        ),
    )(flag, own, near, end, far, *tables)


def rows_tables(place, length, blocks):
    depth = length // RADIX
    per_block = depth // blocks
    p = jnp.arange(depth, dtype=jnp.int32)
    k = jnp.arange(RADIX // 2 + 1, dtype=jnp.int32)
    cosine, sine = unit_angle(k[:, None] * p[None, :], length)
    spread = lambda t: jnp.broadcast_to(t[:, :, None], t.shape + (128,))
    kept = place * per_block + jnp.arange(per_block, dtype=jnp.int32)
    other = jnp.where(place >= blocks // 2, blocks - 1, 0) * per_block + jnp.arange(
        per_block, dtype=jnp.int32
    )
    parts = []
    for shift in (0, 1):
        for which in (kept, other):
            c, s = unit_angle((which[:, None] + shift) * p[None, :], depth)
            sign = -1.0 if shift else 1.0
            parts.append(jnp.concatenate([c, -s * sign], axis=1))
            parts.append(jnp.concatenate([s, c * sign], axis=1))
    return (spread(cosine), spread(sine)) + halves(jnp.concatenate(parts, axis=0))


def columns_kernel(*refs):
    parts = refs[:4]
    cosine, sine, table_high, table_low, out, high, low = refs[4:]
    groups, _, rows, depth = parts[0].shape

    @pl.loop(0, rows // 16)
    def _(step):
        here = pl.ds(pl.multiple_of(step * 16, 16), 16)
        for lane in range(0, depth, 128):
            lanes = pl.ds(lane, 128)
            values = [
                (parts[q % 4][q // 4, 0, here, lanes], parts[q % 4][q // 4, 1, here, lanes])
                for q in range(RADIX)
            ]
            spectrum = small_dft(values, RADIX)
            for k in range(RADIX):
                real, imag = spectrum[k]
                if k:
                    c = cosine[pl.ds(k, 1), lanes]
                    s = sine[pl.ds(k, 1), lanes]
                    real, imag = real * c - imag * s, real * s + imag * c
                split_store(high, low, (k, here, lanes), real)
                split_store(high, low, (k, here, pl.ds(depth + lane, 128)), imag)

    @pl.loop(0, RADIX)
    def _(k):
        result = product(high[k], low[k], table_high[...], table_low[...])
        out[0, k] = result[:, :depth]
        out[1, k] = result[:, depth:]


def columns_stage(parts, length):
    groups, _, rows, depth = parts[0].shape
    p = jnp.arange(depth, dtype=jnp.int32)
    k = jnp.arange(RADIX, dtype=jnp.int32)
    cosine, sine = unit_angle(k[:, None] * p[None, :], length)
    c, s = unit_angle(p[:, None] * p[None, :], depth)
    table = jnp.concatenate(
        [jnp.concatenate([c, s], axis=1), jnp.concatenate([-s, c], axis=1)], axis=0
    )
    tile = 64
    return pl.pallas_call(
        columns_kernel,
        grid=(rows // tile,),
        out_shape=jax.ShapeDtypeStruct((2, RADIX, rows, depth), jnp.float32),
        in_specs=[pl.BlockSpec((groups, 2, tile, depth), lambda i: (0, 0, i, 0))] * 4 + [FULL] * 4,
        out_specs=pl.BlockSpec((2, RADIX, tile, depth), lambda i: (0, 0, i, 0)),
        scratch_shapes=[
            VMEM((RADIX, tile, 2 * depth), jnp.bfloat16),
            VMEM((RADIX, tile, 2 * depth), jnp.bfloat16),
        ],
        compiler_params=pltpu.CompilerParams(vmem_limit_bytes=56 * 2**20),
        cost_estimate=pl.CostEstimate(
            flops=30 * 10**9, bytes_accessed=32 * 2**20, transcendentals=0
        ),
    )(*parts, cosine, sine, *halves(table))


def line_transform(density, kernel_rows, kernel_cols, blocks, groups):
    rows_here, width = density.shape
    length = rows_here * blocks
    columns = width * groups
    place = lax.axis_index("gy")
    upper = place >= 2
    inner = (place == 1) | (place == 2)
    flag = upper.astype(jnp.int32).reshape(1)
    tables = rows_tables(place, length, blocks)
    chunk = columns // RADIX
    parts = []
    for m in range(width // chunk):
        own = density[:, m * chunk : (m + 1) * chunk]
        end = lax.ppermute(own, "gy", [(0, 1), (3, 2)])
        near = lax.ppermute(own, "gy", [(1, 2), (2, 1)])
        far = lax.ppermute(own, "gy", [(0, 2), (3, 1)])
        kept, sent = rows_stage(flag, own, near, end, far, tables)
        given = lax.ppermute(sent, "gy", [(1, 0), (2, 3)])
        mine = jnp.where(inner, kept, given)
        mine = mine.reshape(2, groups, rows_here // groups, chunk).transpose(1, 0, 2, 3)
        parts.append(lax.all_to_all(mine, "gx", split_axis=0, concat_axis=0, tiled=True))
    result = columns_stage(parts, columns)
    rows_part = rows_here // groups
    share = chunk // groups
    result = result.reshape(2, RADIX, rows_part, groups, share).transpose(3, 0, 2, 4, 1)
    result = result.reshape(groups, 2, rows_part, width)
    result = lax.all_to_all(result, "gx", split_axis=0, concat_axis=0, tiled=True)
    result = result.transpose(1, 0, 2, 3).reshape(2, RADIX, rows_here // RADIX, width)
    result = result.transpose(0, 2, 1, 3).reshape(2, rows_here, width)
    factor = kernel_rows[:, None] * kernel_cols[None, :] * (1.0 / math.sqrt(length * columns))
    return (result[0] * factor, result[1] * factor)


def solution(mesh):
    blocks, groups = mesh.shape["gy"], mesh.shape["gx"]

    def body(density, kernel_rows, kernel_cols):
        width = density.shape[1]
        if blocks == 4 and width % 4 == 0 and 4 * groups == RADIX:
            return line_transform(density, kernel_rows, kernel_cols, blocks, groups)
        return on_device(density, kernel_rows, kernel_cols)

    return jax.shard_map(
        body,
        mesh=mesh,
        in_specs=(P("gy", "gx"), P("gy"), P("gx")),
        out_specs=(P("gy", "gx"), P("gy", "gx")),
        check_vma=False,
    )
```

```python
import math

import jax
import jax.numpy as jnp
from jax import lax
from jax.experimental import pallas as pl
from jax.experimental.pallas import tpu as pltpu
from jax.sharding import PartitionSpec as P

NR = 8192
NC = 8192


HIGHEST = lax.Precision.HIGHEST
TWO_PI = 2.0 * math.pi


def dft_tables(length):
    positions = jnp.arange(length, dtype=jnp.int32)
    phase = positions[:, None] * positions[None, :] % length
    phase_angle = phase.astype(jnp.float32) * (-TWO_PI / length)
    return (jnp.cos(phase_angle), jnp.sin(phase_angle))


def rotate_by(real_part, imag_part, cosine, sine_part):
    return (real_part * cosine - imag_part * sine_part, real_part * sine_part + imag_part * cosine)


def rotate_phase(real_part, imag_part, phase, total):
    phase_angle = (phase % total).astype(jnp.float32) * (-TWO_PI / total)
    return rotate_by(real_part, imag_part, jnp.cos(phase_angle), jnp.sin(phase_angle))


def split_length(length):
    inner = 1
    for factor in range(1, length + 1):
        if factor * factor > length:
            break
        if length % factor == 0:
            inner = factor
    return (inner, length // inner)


def whole_columns_dft(real_part):
    rows_here, length = real_part.shape
    inner, outer = split_length(length)
    cos_outer, sin_outer = dft_tables(outer)
    shaped_real = real_part.reshape(rows_here, outer, inner)
    first_real = jnp.einsum("rqp,qk->rkp", shaped_real, cos_outer, precision=HIGHEST)
    first_imag = jnp.einsum("rqp,qk->rkp", shaped_real, sin_outer, precision=HIGHEST)
    phase = (
        jnp.arange(outer, dtype=jnp.int32)[:, None] * jnp.arange(inner, dtype=jnp.int32)[None, :]
    )
    first_real, first_imag = rotate_phase(first_real, first_imag, phase[None, :, :], length)
    cos_inner, sin_inner = dft_tables(inner)
    new_real = jnp.einsum("rkp,pj->rjk", first_real, cos_inner, precision=HIGHEST) - jnp.einsum(
        "rkp,pj->rjk", first_imag, sin_inner, precision=HIGHEST
    )
    new_imag = jnp.einsum("rkp,pj->rjk", first_real, sin_inner, precision=HIGHEST) + jnp.einsum(
        "rkp,pj->rjk", first_imag, cos_inner, precision=HIGHEST
    )
    return (new_real.reshape(rows_here, length), new_imag.reshape(rows_here, length))


def whole_rows_dft(real_part, imag_part):
    length, width_here = real_part.shape
    inner, outer = split_length(length)
    cos_outer, sin_outer = dft_tables(outer)
    shaped_real = real_part.reshape(outer, inner, width_here)
    shaped_imag = imag_part.reshape(outer, inner, width_here)
    first_real = jnp.einsum("qpc,qk->kpc", shaped_real, cos_outer, precision=HIGHEST) - jnp.einsum(
        "qpc,qk->kpc", shaped_imag, sin_outer, precision=HIGHEST
    )
    first_imag = jnp.einsum("qpc,qk->kpc", shaped_real, sin_outer, precision=HIGHEST) + jnp.einsum(
        "qpc,qk->kpc", shaped_imag, cos_outer, precision=HIGHEST
    )
    phase = (
        jnp.arange(outer, dtype=jnp.int32)[:, None] * jnp.arange(inner, dtype=jnp.int32)[None, :]
    )
    first_real, first_imag = rotate_phase(first_real, first_imag, phase[:, :, None], length)
    cos_inner, sin_inner = dft_tables(inner)
    new_real = jnp.einsum("kpc,pj->jkc", first_real, cos_inner, precision=HIGHEST) - jnp.einsum(
        "kpc,pj->jkc", first_imag, sin_inner, precision=HIGHEST
    )
    new_imag = jnp.einsum("kpc,pj->jkc", first_real, sin_inner, precision=HIGHEST) + jnp.einsum(
        "kpc,pj->jkc", first_imag, cos_inner, precision=HIGHEST
    )
    return (new_real.reshape(length, width_here), new_imag.reshape(length, width_here))


def pencil_transform(density):
    rows_here, width_here = density.shape
    row_slab = lax.all_to_all(density, "gx", split_axis=0, concat_axis=1, tiled=True)
    real_part, imag_part = whole_columns_dft(row_slab)
    column_slab = (
        lax.all_to_all(
            lax.all_to_all(real_part, "gx", split_axis=1, concat_axis=0, tiled=True),
            "gy",
            split_axis=1,
            concat_axis=0,
            tiled=True,
        ),
        lax.all_to_all(
            lax.all_to_all(imag_part, "gx", split_axis=1, concat_axis=0, tiled=True),
            "gy",
            split_axis=1,
            concat_axis=0,
            tiled=True,
        ),
    )
    real_part, imag_part = whole_rows_dft(column_slab[0], column_slab[1])
    returned = (
        lax.all_to_all(real_part, "gy", split_axis=0, concat_axis=1, tiled=True),
        lax.all_to_all(imag_part, "gy", split_axis=0, concat_axis=1, tiled=True),
    )
    return (returned[0].reshape(rows_here, width_here), returned[1].reshape(rows_here, width_here))


def on_device(density, kernel_rows, kernel_cols):
    real_part, imag_part = pencil_transform(density)
    factor = kernel_rows[:, None] * kernel_cols[None, :] * (1.0 / math.sqrt(NR * NC))
    return (real_part * factor, imag_part * factor)


RADIX = 32
VMEM = pltpu.VMEM
FULL = pl.BlockSpec(memory_space=pltpu.VMEM)


def unit_angle(index, total):
    angle = (index % total).astype(jnp.float32) * (-TWO_PI / total)
    return (jnp.cos(angle), jnp.sin(angle))


def halves(table):
    high = lax.reduce_precision(table, exponent_bits=8, mantissa_bits=7)
    return (high.astype(jnp.bfloat16), (table - high).astype(jnp.bfloat16))


def times_root(value, index, total):
    real, imag = value
    index = index % total
    if index == 0:
        return value
    if 4 * index == total:
        return (imag, -real) if imag is not None else (None, -real)
    if 2 * index == total:
        return (-real, None if imag is None else -imag)
    cosine = math.cos(TWO_PI * index / total)
    sine = -math.sin(TWO_PI * index / total)
    if imag is None:
        return (real * cosine, real * sine)
    if real is None:
        return (imag * -sine, imag * cosine)
    return (real * cosine - imag * sine, real * sine + imag * cosine)


def plus(left, right):
    if left is None:
        return right
    return left if right is None else left + right


def minus(left, right):
    if right is None:
        return left
    return -right if left is None else left - right


def small_dft(values, needed):
    length = len(values)
    if length == 1:
        return values
    half = length // 2
    keep = min(needed, half)
    even = small_dft(values[0::2], keep)
    odd = small_dft(values[1::2], keep)
    out = [None] * length
    for k in range(keep):
        turned = times_root(odd[k], k, length)
        out[k] = (plus(even[k][0], turned[0]), plus(even[k][1], turned[1]))
        out[k + half] = (minus(even[k][0], turned[0]), minus(even[k][1], turned[1]))
    return out


def real_dft(values):
    length = len(values)
    if length == 1:
        return [(values[0], None)]
    half = length // 2
    even = real_dft(values[0::2])
    odd = real_dft(values[1::2])
    out = [None] * (half + 1)

    def entry(spectrum, k):
        if k < len(spectrum):
            return spectrum[k]
        real, imag = spectrum[half - k]
        return (real, None if imag is None else -imag)

    for k in range(half + 1):
        if k == half:
            e, o = even[0], odd[0]
            out[k] = (minus(e[0], o[0]), None)
        else:
            turned = times_root(entry(odd, k), k, length)
            e = entry(even, k)
            out[k] = (plus(e[0], turned[0]), plus(e[1], turned[1]))
    return out


def product(left_high, left_low, right_high, right_low):
    dot = lambda a, b: jnp.dot(a, b, preferred_element_type=jnp.float32)
    return dot(left_high, right_high) + dot(left_high, right_low) + dot(left_low, right_high)


def split_store(high_ref, low_ref, place, value):
    high = value.astype(jnp.bfloat16)
    high_ref[place] = high
    low_ref[place] = (value - high.astype(jnp.float32)).astype(jnp.bfloat16)


def rows_kernel(flag, own, near, end, far, cosine, sine, table_high, table_low, kept, sent, high, low):
    depth = cosine.shape[1]
    width = own.shape[1]
    per_block = own.shape[0] // depth
    count = RADIX // 2 + 1
    quarter = table_high.shape[0] // 8
    upper = flag[0] > 0

    @pl.loop(0, depth // 16)
    def _(step):
        start = pl.multiple_of(step * 16, 16)
        for lane in range(0, width, 128):
            lanes = pl.ds(lane, 128)

            def take(ref, q):
                return ref[pl.ds(pl.multiple_of(q * depth + start, 16), 16), lanes]

            blocks = []
            for first, second in ((end, far), (own, near), (near, own), (far, end)):
                for q in range(per_block):
                    blocks.append(jnp.where(upper, take(second, q), take(first, q)))
            spectrum = real_dft(blocks)
            for k in range(count):
                real, imag = spectrum[k]
                if k:
                    c = cosine[k, pl.ds(start, 16), :]
                    s = sine[k, pl.ds(start, 16), :]
                    if imag is None:
                        real, imag = real * c, real * s
                    else:
                        real, imag = real * c - imag * s, real * s + imag * c
                if imag is None:
                    imag = jnp.zeros_like(real)
                split_store(high, low, (k, pl.ds(start, 16), lanes), real)
                split_store(high, low, (k, pl.ds(pl.multiple_of(depth + start, 16), 16), lanes), imag)

    def put(k, result):
        rows = pl.ds(pl.multiple_of(k * quarter, 8), quarter)
        kept[0, rows, :] = result[0:quarter]
        kept[1, rows, :] = result[quarter : 2 * quarter]
        sent[0, rows, :] = result[2 * quarter : 3 * quarter]
        sent[1, rows, :] = result[3 * quarter : 4 * quarter]

    direct = pl.ds(0, 4 * quarter)
    for k in (0, RADIX // 2):
        put(k, product(table_high[direct, :], table_low[direct, :], high[k], low[k]))

    @pl.loop(1, RADIX // 2)
    def _(k):
        result = product(table_high[...], table_low[...], high[k], low[k])
        put(k, result[: 4 * quarter])
        put(RADIX - k, result[4 * quarter :])


def rows_stage(flag, own, near, end, far, tables):
    length, width = own.shape
    depth = tables[0].shape[1]
    shape = jax.ShapeDtypeStruct((2, length, width), jnp.float32)
    count = RADIX // 2 + 1
    return pl.pallas_call(
        rows_kernel,
        out_shape=(shape, shape),
        in_specs=[pl.BlockSpec(memory_space=pltpu.SMEM)] + [FULL] * 8,
        out_specs=(FULL, FULL),
        scratch_shapes=[
            VMEM((count, 2 * depth, width), jnp.bfloat16),
            VMEM((count, 2 * depth, width), jnp.bfloat16),
        ],
        compiler_params=pltpu.CompilerParams(vmem_limit_bytes=56 * 2**20),
        cost_estimate=pl.CostEstimate(
            flops=30 * 10**9, bytes_accessed=24 * 2**20, transcendentals=0
        ),
    )(flag, own, near, end, far, *tables)


def rows_tables(place, length, blocks):
    depth = length // RADIX
    per_block = depth // blocks
    p = jnp.arange(depth, dtype=jnp.int32)
    k = jnp.arange(RADIX // 2 + 1, dtype=jnp.int32)
    cosine, sine = unit_angle(k[:, None] * p[None, :], length)
    spread = lambda t: jnp.broadcast_to(t[:, :, None], t.shape + (128,))
    kept = place * per_block + jnp.arange(per_block, dtype=jnp.int32)
    other = jnp.where(place >= blocks // 2, blocks - 1, 0) * per_block + jnp.arange(
        per_block, dtype=jnp.int32
    )
    parts = []
    for shift in (0, 1):
        for which in (kept, other):
            c, s = unit_angle((which[:, None] + shift) * p[None, :], depth)
            sign = -1.0 if shift else 1.0
            parts.append(jnp.concatenate([c, -s * sign], axis=1))
            parts.append(jnp.concatenate([s, c * sign], axis=1))
    return (spread(cosine), spread(sine)) + halves(jnp.concatenate(parts, axis=0))


def columns_kernel(*refs):
    parts = refs[:-7]
    cosine, sine, table_high, table_low, out, high, low = refs[-7:]
    rows = parts[0].shape[2]
    depth = cosine.shape[1]
    pieces = [(m, lane) for m in range(len(parts)) for lane in range(0, parts[m].shape[3], 128)]
    per_group = depth // 128

    @pl.loop(0, rows // 16)
    def _(step):
        start = pl.multiple_of(step * 16, 16)
        here = pl.ds(start, 16)
        for lane in range(0, depth, 128):
            lanes = pl.ds(lane, 128)
            values = []
            for q in range(RADIX):
                m, offset = pieces[q % 4 * per_group + lane // 128]
                values.append(
                    tuple(parts[m][q // 4, t, here, pl.ds(offset, 128)] for t in range(2))
                )
            spectrum = small_dft(values, RADIX)
            for k in range(RADIX):
                real, imag = spectrum[k]
                if k:
                    c = cosine[pl.ds(k, 1), lanes]
                    s = sine[pl.ds(k, 1), lanes]
                    real, imag = real * c - imag * s, real * s + imag * c
                there = pl.ds(pl.multiple_of(k * rows + start, 16), 16)
                split_store(high, low, (there, lanes), real)
                split_store(high, low, (there, pl.ds(depth + lane, 128)), imag)

    some = 8

    @pl.loop(0, RADIX // some)
    def _(k):
        here = pl.ds(pl.multiple_of(k * some * rows, 16), some * rows)
        result = product(high[here, :], low[here, :], table_high[...], table_low[...])
        out[0, here, :] = result[:, :depth]
        out[1, here, :] = result[:, depth:]


def columns_tables(length):
    depth = length // RADIX
    p = jnp.arange(depth, dtype=jnp.int32)
    k = jnp.arange(RADIX, dtype=jnp.int32)
    cosine, sine = unit_angle(k[:, None] * p[None, :], length)
    c, s = unit_angle(p[:, None] * p[None, :], depth)
    table = jnp.concatenate(
        [jnp.concatenate([c, s], axis=1), jnp.concatenate([-s, c], axis=1)], axis=0
    )
    return (cosine, sine) + halves(table)


def columns_stage(parts, tables, piece, tile):
    groups = parts[0].shape[0]
    depth = tables[0].shape[1]
    return pl.pallas_call(
        columns_kernel,
        grid=(1,),
        out_shape=jax.ShapeDtypeStruct((2, RADIX * tile, depth), jnp.float32),
        in_specs=[
            pl.BlockSpec((groups, 2, tile, part.shape[3]), lambda i: (0, 0, piece, 0))
            for part in parts
        ]
        + [FULL] * 4,
        out_specs=pl.BlockSpec((2, RADIX * tile, depth), lambda i: (0, 0, 0)),
        scratch_shapes=[
            VMEM((RADIX * tile, 2 * depth), jnp.bfloat16),
            VMEM((RADIX * tile, 2 * depth), jnp.bfloat16),
        ],
        compiler_params=pltpu.CompilerParams(vmem_limit_bytes=56 * 2**20),
        cost_estimate=pl.CostEstimate(
            flops=8 * 10**9, bytes_accessed=8 * 2**20, transcendentals=0
        ),
    )(*parts, *tables)


def finish_kernel(*refs):
    pieces = refs[:-4]
    by_row, by_column, real_out, imag_out = refs[-4:]
    groups, _, some, width = pieces[0].shape
    count = groups * len(pieces)
    for t, out in enumerate((real_out, imag_out)):
        for lane in range(0, width, 128):
            lanes = pl.ds(lane, 128)
            rows = [pieces[k % len(pieces)][k // len(pieces), t, :, lanes] for k in range(count)]
            turned = jnp.transpose(jnp.stack(rows, axis=0), (1, 0, 2))
            turned = turned.reshape(some * count, 128)
            out[:, lanes] = turned * (by_row[...] * by_column[:, lanes])


def finish_stage(pieces, by_row, by_column):
    groups, _, rows, width = pieces[0].shape
    some = 8
    tall = some * groups * len(pieces)
    shape = jax.ShapeDtypeStruct((rows * groups * len(pieces), width), jnp.float32)
    out_spec = pl.BlockSpec((tall, width), lambda i: (i, 0))
    return pl.pallas_call(
        finish_kernel,
        grid=(rows // some,),
        out_shape=(shape, shape),
        in_specs=[pl.BlockSpec((groups, 2, some, width), lambda i: (0, 0, i, 0))] * len(pieces)
        + [pl.BlockSpec((tall, 128), lambda i: (i, 0)), pl.BlockSpec((1, width), lambda i: (0, 0))],
        out_specs=(out_spec, out_spec),
        compiler_params=pltpu.CompilerParams(vmem_limit_bytes=48 * 2**20),
    )(*pieces, by_row, by_column)


def line_transform(density, kernel_rows, kernel_cols, blocks, groups):
    rows_here, width = density.shape
    length = rows_here * blocks
    columns = width * groups
    place = lax.axis_index("gy")
    upper = place >= 2
    inner = (place == 1) | (place == 2)
    flag = upper.astype(jnp.int32).reshape(1)
    tables = rows_tables(place, length, blocks)
    chunk = columns // RADIX
    parts = []
    begin = 0
    for size in [chunk] * (width // chunk - 1) + [chunk // 2] * 2:
        own = density[:, begin : begin + size]
        begin += size
        end = lax.ppermute(own, "gy", [(0, 1), (3, 2)])
        near = lax.ppermute(own, "gy", [(1, 2), (2, 1)])
        far = lax.ppermute(own, "gy", [(0, 2), (3, 1)])
        kept, sent = rows_stage(flag, own, near, end, far, tables)
        given = lax.ppermute(sent, "gy", [(1, 0), (2, 3)])
        mine = jnp.where(inner, kept, given)
        mine = mine.reshape(2, groups, rows_here // groups, size).transpose(1, 0, 2, 3)
        parts.append(lax.all_to_all(mine, "gx", split_axis=0, concat_axis=0, tiled=True))
    rows_part = rows_here // groups
    share = chunk // groups
    tile = rows_here // RADIX
    tables = columns_tables(columns)
    pieces = []
    for piece in range(rows_part // tile):
        result = columns_stage(parts, tables, piece, tile)
        result = result.reshape(2, RADIX, tile, groups, share).transpose(3, 0, 2, 4, 1)
        result = result.reshape(groups, 2, tile, width)
        pieces.append(lax.all_to_all(result, "gx", split_axis=0, concat_axis=0, tiled=True))
    scale = kernel_rows * (1.0 / math.sqrt(length * columns))
    by_row = jnp.broadcast_to(scale[:, None], (rows_here, 128))
    return finish_stage(pieces, by_row, kernel_cols[None, :])


def solution(mesh):
    blocks, groups = mesh.shape["gy"], mesh.shape["gx"]

    def body(density, kernel_rows, kernel_cols):
        width = density.shape[1]
        if blocks == 4 and width % 4 == 0 and 4 * groups == RADIX:
            return line_transform(density, kernel_rows, kernel_cols, blocks, groups)
        return on_device(density, kernel_rows, kernel_cols)

    return jax.shard_map(
        body,
        mesh=mesh,
        in_specs=(P("gy", "gx"), P("gy"), P("gx")),
        out_specs=(P("gy", "gx"), P("gy", "gx")),
        check_vma=False,
    )
```

```python
import math

import jax
import jax.numpy as jnp
from jax import lax
from jax.experimental import pallas as pl
from jax.experimental.pallas import tpu as pltpu
from jax.sharding import PartitionSpec as P

NR = 8192
NC = 8192


HIGHEST = lax.Precision.HIGHEST
TWO_PI = 2.0 * math.pi


def dft_tables(length):
    positions = jnp.arange(length, dtype=jnp.int32)
    phase = positions[:, None] * positions[None, :] % length
    phase_angle = phase.astype(jnp.float32) * (-TWO_PI / length)
    return (jnp.cos(phase_angle), jnp.sin(phase_angle))


def rotate_by(real_part, imag_part, cosine, sine_part):
    return (real_part * cosine - imag_part * sine_part, real_part * sine_part + imag_part * cosine)


def rotate_phase(real_part, imag_part, phase, total):
    phase_angle = (phase % total).astype(jnp.float32) * (-TWO_PI / total)
    return rotate_by(real_part, imag_part, jnp.cos(phase_angle), jnp.sin(phase_angle))


def split_length(length):
    inner = 1
    for factor in range(1, length + 1):
        if factor * factor > length:
            break
        if length % factor == 0:
            inner = factor
    return (inner, length // inner)


def whole_columns_dft(real_part):
    rows_here, length = real_part.shape
    inner, outer = split_length(length)
    cos_outer, sin_outer = dft_tables(outer)
    shaped_real = real_part.reshape(rows_here, outer, inner)
    first_real = jnp.einsum("rqp,qk->rkp", shaped_real, cos_outer, precision=HIGHEST)
    first_imag = jnp.einsum("rqp,qk->rkp", shaped_real, sin_outer, precision=HIGHEST)
    phase = (
        jnp.arange(outer, dtype=jnp.int32)[:, None] * jnp.arange(inner, dtype=jnp.int32)[None, :]
    )
    first_real, first_imag = rotate_phase(first_real, first_imag, phase[None, :, :], length)
    cos_inner, sin_inner = dft_tables(inner)
    new_real = jnp.einsum("rkp,pj->rjk", first_real, cos_inner, precision=HIGHEST) - jnp.einsum(
        "rkp,pj->rjk", first_imag, sin_inner, precision=HIGHEST
    )
    new_imag = jnp.einsum("rkp,pj->rjk", first_real, sin_inner, precision=HIGHEST) + jnp.einsum(
        "rkp,pj->rjk", first_imag, cos_inner, precision=HIGHEST
    )
    return (new_real.reshape(rows_here, length), new_imag.reshape(rows_here, length))


def whole_rows_dft(real_part, imag_part):
    length, width_here = real_part.shape
    inner, outer = split_length(length)
    cos_outer, sin_outer = dft_tables(outer)
    shaped_real = real_part.reshape(outer, inner, width_here)
    shaped_imag = imag_part.reshape(outer, inner, width_here)
    first_real = jnp.einsum("qpc,qk->kpc", shaped_real, cos_outer, precision=HIGHEST) - jnp.einsum(
        "qpc,qk->kpc", shaped_imag, sin_outer, precision=HIGHEST
    )
    first_imag = jnp.einsum("qpc,qk->kpc", shaped_real, sin_outer, precision=HIGHEST) + jnp.einsum(
        "qpc,qk->kpc", shaped_imag, cos_outer, precision=HIGHEST
    )
    phase = (
        jnp.arange(outer, dtype=jnp.int32)[:, None] * jnp.arange(inner, dtype=jnp.int32)[None, :]
    )
    first_real, first_imag = rotate_phase(first_real, first_imag, phase[:, :, None], length)
    cos_inner, sin_inner = dft_tables(inner)
    new_real = jnp.einsum("kpc,pj->jkc", first_real, cos_inner, precision=HIGHEST) - jnp.einsum(
        "kpc,pj->jkc", first_imag, sin_inner, precision=HIGHEST
    )
    new_imag = jnp.einsum("kpc,pj->jkc", first_real, sin_inner, precision=HIGHEST) + jnp.einsum(
        "kpc,pj->jkc", first_imag, cos_inner, precision=HIGHEST
    )
    return (new_real.reshape(length, width_here), new_imag.reshape(length, width_here))


def pencil_transform(density):
    rows_here, width_here = density.shape
    row_slab = lax.all_to_all(density, "gx", split_axis=0, concat_axis=1, tiled=True)
    real_part, imag_part = whole_columns_dft(row_slab)
    column_slab = (
        lax.all_to_all(
            lax.all_to_all(real_part, "gx", split_axis=1, concat_axis=0, tiled=True),
            "gy",
            split_axis=1,
            concat_axis=0,
            tiled=True,
        ),
        lax.all_to_all(
            lax.all_to_all(imag_part, "gx", split_axis=1, concat_axis=0, tiled=True),
            "gy",
            split_axis=1,
            concat_axis=0,
            tiled=True,
        ),
    )
    real_part, imag_part = whole_rows_dft(column_slab[0], column_slab[1])
    returned = (
        lax.all_to_all(real_part, "gy", split_axis=0, concat_axis=1, tiled=True),
        lax.all_to_all(imag_part, "gy", split_axis=0, concat_axis=1, tiled=True),
    )
    return (returned[0].reshape(rows_here, width_here), returned[1].reshape(rows_here, width_here))


def on_device(density, kernel_rows, kernel_cols):
    real_part, imag_part = pencil_transform(density)
    factor = kernel_rows[:, None] * kernel_cols[None, :] * (1.0 / math.sqrt(NR * NC))
    return (real_part * factor, imag_part * factor)


RADIX = 32
VMEM = pltpu.VMEM
FULL = pl.BlockSpec(memory_space=pltpu.VMEM)


def unit_angle(index, total):
    angle = (index % total).astype(jnp.float32) * (-TWO_PI / total)
    return (jnp.cos(angle), jnp.sin(angle))


def halves(table):
    high = lax.reduce_precision(table, exponent_bits=8, mantissa_bits=7)
    return (high.astype(jnp.bfloat16), (table - high).astype(jnp.bfloat16))


def times_root(value, index, total):
    real, imag = value
    index = index % total
    if index == 0:
        return value
    if 4 * index == total:
        return (imag, -real) if imag is not None else (None, -real)
    if 2 * index == total:
        return (-real, None if imag is None else -imag)
    cosine = math.cos(TWO_PI * index / total)
    sine = -math.sin(TWO_PI * index / total)
    if imag is None:
        return (real * cosine, real * sine)
    if real is None:
        return (imag * -sine, imag * cosine)
    return (real * cosine - imag * sine, real * sine + imag * cosine)


def plus(left, right):
    if left is None:
        return right
    return left if right is None else left + right


def minus(left, right):
    if right is None:
        return left
    return -right if left is None else left - right


def small_dft(values, needed):
    length = len(values)
    if length == 1:
        return values
    half = length // 2
    keep = min(needed, half)
    even = small_dft(values[0::2], keep)
    odd = small_dft(values[1::2], keep)
    out = [None] * length
    for k in range(keep):
        turned = times_root(odd[k], k, length)
        out[k] = (plus(even[k][0], turned[0]), plus(even[k][1], turned[1]))
        out[k + half] = (minus(even[k][0], turned[0]), minus(even[k][1], turned[1]))
    return out


def real_dft(values):
    length = len(values)
    if length == 1:
        return [(values[0], None)]
    half = length // 2
    even = real_dft(values[0::2])
    odd = real_dft(values[1::2])
    out = [None] * (half + 1)

    def entry(spectrum, k):
        if k < len(spectrum):
            return spectrum[k]
        real, imag = spectrum[half - k]
        return (real, None if imag is None else -imag)

    for k in range(half + 1):
        if k == half:
            e, o = even[0], odd[0]
            out[k] = (minus(e[0], o[0]), None)
        else:
            turned = times_root(entry(odd, k), k, length)
            e = entry(even, k)
            out[k] = (plus(e[0], turned[0]), plus(e[1], turned[1]))
    return out


def product(left_high, left_low, right_high, right_low):
    dot = lambda a, b: jnp.dot(a, b, preferred_element_type=jnp.float32)
    return dot(left_high, right_high) + dot(left_high, right_low) + dot(left_low, right_high)


def split_store(high_ref, low_ref, place, value):
    high = value.astype(jnp.bfloat16)
    high_ref[place] = high
    low_ref[place] = (value - high.astype(jnp.float32)).astype(jnp.bfloat16)


def rows_kernel(flag, own, near, end, far, cosine, sine, table_high, table_low, kept, sent, high, low):
    depth = cosine.shape[1]
    width = own.shape[1]
    per_block = own.shape[0] // depth
    count = RADIX // 2 + 1
    quarter = table_high.shape[0] // 8
    upper = flag[0] > 0

    @pl.loop(0, depth // 16)
    def _(step):
        start = pl.multiple_of(step * 16, 16)
        for lane in range(0, width, 128):
            lanes = pl.ds(lane, 128)

            def take(ref, q):
                return ref[pl.ds(pl.multiple_of(q * depth + start, 16), 16), lanes]

            blocks = []
            for first, second in ((end, far), (own, near), (near, own), (far, end)):
                for q in range(per_block):
                    blocks.append(jnp.where(upper, take(second, q), take(first, q)))
            spectrum = real_dft(blocks)
            for k in range(count):
                real, imag = spectrum[k]
                if k:
                    c = cosine[k, pl.ds(start, 16), :]
                    s = sine[k, pl.ds(start, 16), :]
                    if imag is None:
                        real, imag = real * c, real * s
                    else:
                        real, imag = real * c - imag * s, real * s + imag * c
                if imag is None:
                    imag = jnp.zeros_like(real)
                split_store(high, low, (k, pl.ds(start, 16), lanes), real)
                split_store(high, low, (k, pl.ds(pl.multiple_of(depth + start, 16), 16), lanes), imag)

    def put(k, result):
        rows = pl.ds(pl.multiple_of(k * quarter, 8), quarter)
        kept[0, rows, :] = result[0:quarter]
        kept[1, rows, :] = result[quarter : 2 * quarter]
        sent[0, rows, :] = result[2 * quarter : 3 * quarter]
        sent[1, rows, :] = result[3 * quarter : 4 * quarter]

    direct = pl.ds(0, 4 * quarter)
    for k in (0, RADIX // 2):
        put(k, product(table_high[direct, :], table_low[direct, :], high[k], low[k]))

    @pl.loop(1, RADIX // 2)
    def _(k):
        result = product(table_high[...], table_low[...], high[k], low[k])
        put(k, result[: 4 * quarter])
        put(RADIX - k, result[4 * quarter :])


def rows_stage(flag, own, near, end, far, tables):
    length, width = own.shape
    depth = tables[0].shape[1]
    shape = jax.ShapeDtypeStruct((2, length, width), jnp.float32)
    count = RADIX // 2 + 1
    return pl.pallas_call(
        rows_kernel,
        out_shape=(shape, shape),
        in_specs=[pl.BlockSpec(memory_space=pltpu.SMEM)] + [FULL] * 8,
        out_specs=(FULL, FULL),
        scratch_shapes=[
            VMEM((count, 2 * depth, width), jnp.bfloat16),
            VMEM((count, 2 * depth, width), jnp.bfloat16),
        ],
        compiler_params=pltpu.CompilerParams(vmem_limit_bytes=56 * 2**20),
        cost_estimate=pl.CostEstimate(
            flops=30 * 10**9, bytes_accessed=24 * 2**20, transcendentals=0
        ),
    )(flag, own, near, end, far, *tables)


def rows_tables(place, length, blocks):
    depth = length // RADIX
    per_block = depth // blocks
    p = jnp.arange(depth, dtype=jnp.int32)
    k = jnp.arange(RADIX // 2 + 1, dtype=jnp.int32)
    cosine, sine = unit_angle(k[:, None] * p[None, :], length)
    spread = lambda t: jnp.broadcast_to(t[:, :, None], t.shape + (128,))
    kept = place * per_block + jnp.arange(per_block, dtype=jnp.int32)
    other = jnp.where(place >= blocks // 2, blocks - 1, 0) * per_block + jnp.arange(
        per_block, dtype=jnp.int32
    )
    parts = []
    for shift in (0, 1):
        for which in (kept, other):
            c, s = unit_angle((which[:, None] + shift) * p[None, :], depth)
            sign = -1.0 if shift else 1.0
            parts.append(jnp.concatenate([c, -s * sign], axis=1))
            parts.append(jnp.concatenate([s, c * sign], axis=1))
    return (spread(cosine), spread(sine)) + halves(jnp.concatenate(parts, axis=0))


def columns_kernel(*refs):
    parts = refs[:-7]
    cosine, sine, table_high, table_low, out, high, low = refs[-7:]
    rows = parts[0].shape[2]
    depth = cosine.shape[1]
    pieces = [(m, lane) for m in range(len(parts)) for lane in range(0, parts[m].shape[3], 128)]
    per_group = depth // 128

    @pl.loop(0, rows // 16)
    def _(step):
        start = pl.multiple_of(step * 16, 16)
        here = pl.ds(start, 16)
        for lane in range(0, depth, 128):
            lanes = pl.ds(lane, 128)
            values = []
            for q in range(RADIX):
                m, offset = pieces[q % 4 * per_group + lane // 128]
                values.append(
                    tuple(parts[m][q // 4, t, here, pl.ds(offset, 128)] for t in range(2))
                )
            spectrum = small_dft(values, RADIX)
            for k in range(RADIX):
                real, imag = spectrum[k]
                if k:
                    c = cosine[pl.ds(k, 1), lanes]
                    s = sine[pl.ds(k, 1), lanes]
                    real, imag = real * c - imag * s, real * s + imag * c
                there = pl.ds(pl.multiple_of(k * rows + start, 16), 16)
                split_store(high, low, (there, lanes), real)
                split_store(high, low, (there, pl.ds(depth + lane, 128)), imag)

    some = 8

    @pl.loop(0, RADIX // some)
    def _(k):
        here = pl.ds(pl.multiple_of(k * some * rows, 16), some * rows)
        result = product(high[here, :], low[here, :], table_high[...], table_low[...])
        out[0, here, :] = result[:, :depth]
        out[1, here, :] = result[:, depth:]


def columns_tables(length):
    depth = length // RADIX
    p = jnp.arange(depth, dtype=jnp.int32)
    k = jnp.arange(RADIX, dtype=jnp.int32)
    cosine, sine = unit_angle(k[:, None] * p[None, :], length)
    c, s = unit_angle(p[:, None] * p[None, :], depth)
    table = jnp.concatenate(
        [jnp.concatenate([c, s], axis=1), jnp.concatenate([-s, c], axis=1)], axis=0
    )
    return (cosine, sine) + halves(table)


def columns_stage(parts, tables, piece, tile):
    groups = parts[0].shape[0]
    depth = tables[0].shape[1]
    return pl.pallas_call(
        columns_kernel,
        grid=(1,),
        out_shape=jax.ShapeDtypeStruct((2, RADIX * tile, depth), jnp.float32),
        in_specs=[
            pl.BlockSpec((groups, 2, tile, part.shape[3]), lambda i: (0, 0, piece, 0))
            for part in parts
        ]
        + [FULL] * 4,
        out_specs=pl.BlockSpec((2, RADIX * tile, depth), lambda i: (0, 0, 0)),
        scratch_shapes=[
            VMEM((RADIX * tile, 2 * depth), jnp.bfloat16),
            VMEM((RADIX * tile, 2 * depth), jnp.bfloat16),
        ],
        compiler_params=pltpu.CompilerParams(vmem_limit_bytes=56 * 2**20),
        cost_estimate=pl.CostEstimate(
            flops=8 * 10**9, bytes_accessed=8 * 2**20, transcendentals=0
        ),
    )(*parts, *tables)


def finish_kernel(*refs):
    pieces = refs[:-4]
    by_row, by_column, real_out, imag_out = refs[-4:]
    groups, _, some, width = pieces[0].shape
    count = groups * len(pieces)
    for t, out in enumerate((real_out, imag_out)):
        for lane in range(0, width, 128):
            lanes = pl.ds(lane, 128)
            rows = [pieces[k % len(pieces)][k // len(pieces), t, :, lanes] for k in range(count)]
            turned = jnp.transpose(jnp.stack(rows, axis=0), (1, 0, 2))
            turned = turned.reshape(some * count, 128)
            out[:, lanes] = turned * (by_row[...] * by_column[:, lanes])


def finish_stage(pieces, by_row, by_column):
    groups, _, rows, width = pieces[0].shape
    some = 8
    tall = some * groups * len(pieces)
    shape = jax.ShapeDtypeStruct((rows * groups * len(pieces), width), jnp.float32)
    out_spec = pl.BlockSpec((tall, width), lambda i: (i, 0))
    return pl.pallas_call(
        finish_kernel,
        grid=(rows // some,),
        out_shape=(shape, shape),
        in_specs=[pl.BlockSpec((groups, 2, some, width), lambda i: (0, 0, i, 0))] * len(pieces)
        + [pl.BlockSpec((tall, 128), lambda i: (i, 0)), pl.BlockSpec((1, width), lambda i: (0, 0))],
        out_specs=(out_spec, out_spec),
        compiler_params=pltpu.CompilerParams(vmem_limit_bytes=48 * 2**20),
    )(*pieces, by_row, by_column)


def line_transform(density, kernel_rows, kernel_cols, blocks, groups):
    rows_here, width = density.shape
    length = rows_here * blocks
    columns = width * groups
    place = lax.axis_index("gy")
    upper = place >= 2
    inner = (place == 1) | (place == 2)
    flag = upper.astype(jnp.int32).reshape(1)
    tables = rows_tables(place, length, blocks)
    chunk = columns // RADIX
    parts = []
    arrived = []
    begin = 0
    for size in [chunk] * (width // chunk - 1) + [chunk // 2] * 2:
        own = density[:, begin : begin + size]
        begin += size
        if len(arrived) > 1:
            own = lax.optimization_barrier((own,) + arrived[-2])[0]
        end = lax.ppermute(own, "gy", [(0, 1), (3, 2)])
        near = lax.ppermute(own, "gy", [(1, 2), (2, 1)])
        far = lax.ppermute(own, "gy", [(0, 2), (3, 1)])
        arrived.append((near, far))
        kept, sent = rows_stage(flag, own, near, end, far, tables)
        given = lax.ppermute(sent, "gy", [(1, 0), (2, 3)])
        mine = jnp.where(inner, kept, given)
        mine = mine.reshape(2, groups, rows_here // groups, size).transpose(1, 0, 2, 3)
        parts.append(lax.all_to_all(mine, "gx", split_axis=0, concat_axis=0, tiled=True))
    rows_part = rows_here // groups
    share = chunk // groups
    tile = rows_here // RADIX
    tables = columns_tables(columns)
    pieces = []
    for piece in range(rows_part // tile):
        result = columns_stage(parts, tables, piece, tile)
        result = result.reshape(2, RADIX, tile, groups, share).transpose(3, 0, 2, 4, 1)
        result = result.reshape(groups, 2, tile, width)
        pieces.append(lax.all_to_all(result, "gx", split_axis=0, concat_axis=0, tiled=True))
    scale = kernel_rows * (1.0 / math.sqrt(length * columns))
    by_row = jnp.broadcast_to(scale[:, None], (rows_here, 128))
    return finish_stage(pieces, by_row, kernel_cols[None, :])


def solution(mesh):
    blocks, groups = mesh.shape["gy"], mesh.shape["gx"]

    def body(density, kernel_rows, kernel_cols):
        width = density.shape[1]
        if blocks == 4 and width % 4 == 0 and 4 * groups == RADIX:
            return line_transform(density, kernel_rows, kernel_cols, blocks, groups)
        return on_device(density, kernel_rows, kernel_cols)

    return jax.shard_map(
        body,
        mesh=mesh,
        in_specs=(P("gy", "gx"), P("gy"), P("gx")),
        out_specs=(P("gy", "gx"), P("gy", "gx")),
        check_vma=False,
    )
```
